32 devices in a mesh: region: 8 (over z, x), pair: 4 (over y, core).
Axes of the slice: x: 2, y: 2, z: 4, core: 2. Of those that a mesh axis runs over, the one named last changes fastest.
Arguments:
- phi: bfloat16 [1024, 8, 32, 128], P('region', None, 'pair'), may hold values from -0.375 to 0.375
- potential: float32 [8, 32, 128], P('region', 'pair'), may hold values from -2 to 2
- pair_list: int32 [32, 2], replicated, may hold values from 0 to 7, as said below
- support: int32 [8, 8], replicated, may hold values 0 or 1
Outputs:
- intersection: float32 [32, 16384], P('pair', 'region')
- hamiltonian: float32 [32, 16384], P('pair', 'region')
- hphi: bfloat16 [1024, 8, 32, 128], P('region', None, 'pair')
The draws below stay inside these ranges and needn't reach their ends.
Inputs may be any that keep to these rules, and one draw needn't show every extreme that they name: `pair_list`: each row is an ordered pair of block numbers; no pair appears twice.
All inputs are finite; a program needn't handle non-finite values.
Results may differ from the reference program's by a relative error of at most 0.0029.
Values may be sent and summed in bfloat16 or wider, within the bound.
A program may use at most 64 MiB of HBM per device.

```python
import jax
import jax.numpy as jnp
from jax import lax

W = 128
NBLK = 8
PLANES = 1
PY = 32
PZ = 128
M = 1024
X = 8
NPAIRS = 32
N_REGION = 8


def draw_pair_list(key, part):
    key_order, key_slot = jax.random.split(key)
    order = jax.random.permutation(key_order, NBLK * NBLK)
    target = (NBLK - 1) * NBLK
    slot = jax.random.randint(key_slot, (), 0, NPAIRS)
    order = jnp.where(order == target, order[slot], order)
    order = order.at[slot].set(target)
    chosen = order[:NPAIRS]
    return jnp.stack([chosen // NBLK, chosen % NBLK], axis=1).astype(jnp.int32)


def with_ends(array, stream_key, least, largest):
    dims = array.shape
    spot = [jax.random.randint(jax.random.fold_in(stream_key, axis), (), 0, dims[axis]) for axis in range(len(dims))]
    array = array.at[tuple(spot)].set(least)
    longest = dims.index(max(dims))
    spot[longest] = (spot[longest] + 1) % dims[longest]
    return array.at[tuple(spot)].set(largest)


def levels(own_key, extent, pieces, least, largest):
    loudness, own = 1.0, jax.random.fold_in(own_key, 6)
    for position, blocks in pieces:
        heights = jnp.exp(jax.random.uniform(jax.random.fold_in(own, position), (blocks,), jnp.float32, least / len(pieces), largest / len(pieces)))
        loudness = loudness * jnp.repeat(heights, extent[position] // blocks).reshape([-1 if axis == position else 1 for axis in range(len(extent))])
    return loudness


def normal_values(own_key, shape, scale, bound, cuts=(), held_as=jnp.bfloat16):
    array = jax.random.normal(own_key, shape, jnp.float32) * scale
    if len(cuts) > 0:
        array = levels(own_key, shape, cuts, -0.22, 0.18) * array
    return jnp.clip(array, min=-bound, max=bound).astype(held_as)


def setup_inputs(seed: int = 0) -> dict:
    arg_keys = jax.random.split(jax.random.key(seed), 5)
    return {
        "phi": normal_values(arg_keys[0], (M, X, PY, PZ), (X * PY) ** -0.5, 0.375, ((0, 8), (2, 4))),
        "potential": jnp.clip(jax.random.uniform(arg_keys[1], (X, PY, PZ), jnp.float32, -2.0, 2.0) * levels(arg_keys[1], (X, PY, PZ), ((0, 8), (1, 4)), -0.4, 0.0), -2.0, 2.0),
        "pair_list": draw_pair_list(jax.random.fold_in(arg_keys[4], 71), 0),
        "support": with_ends((jax.random.randint(arg_keys[3], (NBLK, N_REGION), 0, 2) < 1).astype(jnp.int32), jax.random.fold_in(arg_keys[3], 1), 0, 1),
    }


def apply_block(values_low, potential, keep_mask):
    values = values_low.astype(jnp.float32)
    laplace_sum = jnp.roll(values, -1, axis=1) + jnp.roll(values, 1, axis=1) - 6.0 * values
    laplace_sum = laplace_sum + jnp.roll(values, -1, axis=2) + jnp.roll(values, 1, axis=2)
    z_padded = jnp.pad(values, ((0, 0), (0, 0), (0, 0), (1, 1)))
    laplace_sum = laplace_sum + z_padded[..., 2:] + z_padded[..., :-2]
    applied = (-0.5 * laplace_sum + potential[None] * values) * keep_mask[:, :, None, None]
    return applied.astype(jnp.bfloat16)


def reference(phi, potential, pair_list, support):
    live_mask = jnp.repeat(jnp.repeat(support, W, axis=0), PLANES, axis=1)
    confined = jnp.where(live_mask[:, :, None, None] > 0, phi, jnp.zeros_like(phi))
    keep_mask = live_mask.astype(jnp.float32)
    applied = lax.map(lambda members: apply_block(members[0], potential, members[1]),
                      (confined.reshape(NBLK, W, X, PY, PZ), keep_mask.reshape(NBLK, W, X)))
    applied = applied.reshape(M, X, PY, PZ)
    flat_data = confined.reshape(M, X * PY * PZ)
    flat_applied = applied.reshape(M, X * PY * PZ)
    contract_dims = (((1,), (1,)), ((), ()))

    def pair_terms(pair_row):
        first_row = (pair_row[0] * W).astype(jnp.int32)
        second_row = (pair_row[1] * W).astype(jnp.int32)
        left_rows = lax.dynamic_slice_in_dim(flat_data, first_row, W, 0)
        right_rows = lax.dynamic_slice_in_dim(flat_data, second_row, W, 0)
        ham_rows = lax.dynamic_slice_in_dim(flat_applied, second_row, W, 0)
        return (lax.dot_general(left_rows, right_rows, contract_dims, preferred_element_type=jnp.float32),
                lax.dot_general(left_rows, ham_rows, contract_dims, preferred_element_type=jnp.float32))

    intersection, hamiltonian = lax.map(pair_terms, pair_list)
    return intersection.reshape(NPAIRS, W * W), hamiltonian.reshape(NPAIRS, W * W), applied
```

```python
import jax
import jax.numpy as jnp
from jax import lax
from jax.experimental import pallas as pl
from jax.experimental.pallas import tpu as pltpu
from jax.sharding import PartitionSpec as P

W = 128


def pair_kernel(pairs_ref, data_ref, applied_ref, out_ref):
    contract = (((1,), (1,)), ((), ()))

    def step(k, carry):
        left = data_ref[pl.ds(pl.multiple_of(pairs_ref[k, 0] * W, W), W), :]
        rows = pl.ds(pl.multiple_of(pairs_ref[k, 1] * W, W), W)
        right = jnp.concatenate([data_ref[rows, :], applied_ref[rows, :]], axis=0)
        both = lax.dot_general(left, right, contract, preferred_element_type=jnp.float32)
        out_ref[k, 0] = both[:, :W]
        out_ref[k, 1] = both[:, W:]
        return carry

    lax.fori_loop(0, pairs_ref.shape[0], step, 0)


def pair_blocks(pair_list, data, applied):
    count = pair_list.shape[0]
    return pl.pallas_call(
        pair_kernel,
        out_shape=jax.ShapeDtypeStruct((count, 2, W, W), jnp.float32),
        in_specs=[
            pl.BlockSpec(memory_space=pltpu.SMEM),
            pl.BlockSpec(memory_space=pltpu.VMEM),
            pl.BlockSpec(memory_space=pltpu.VMEM),
        ],
        out_specs=pl.BlockSpec(memory_space=pltpu.VMEM),
        compiler_params=pltpu.CompilerParams(vmem_limit_bytes=32 * 2**20),
        cost_estimate=pl.CostEstimate(
            flops=count * 4 * W * W * data.shape[1],
            bytes_accessed=data.size * 4 + count * 8 * W * W,
            transcendentals=0,
        ),
    )(pair_list, data, applied)


def local(phi, potential, pair_list, support):
    region_id = lax.axis_index("region")
    region_count = lax.axis_size("region")
    pair_axis = lax.axis_size("pair")
    func_count, _, row_count, depth = phi.shape
    owners = (region_id * func_count + jnp.arange(func_count)) // W
    live = support[owners]
    confined = jnp.where((live > 0)[:, :, None, None], phi, jnp.zeros_like(phi))
    forward = [(i, (i + 1) % pair_axis) for i in range(pair_axis)]
    backward = [(target, source) for source, target in forward]
    low = lax.ppermute(confined[:, :, -1:], "pair", forward)
    high = lax.ppermute(confined[:, :, :1], "pair", backward)
    grid_potential = lax.all_gather(potential, "region", axis=0, tiled=True)
    data = lax.all_to_all(confined, "region", split_axis=1, concat_axis=0, tiled=True)

    center = confined.astype(jnp.float32)
    total = jnp.roll(center, -1, axis=1) + jnp.roll(center, 1, axis=1) - 6.0 * center
    below = jnp.concatenate([low.astype(jnp.float32), center[:, :, :-1]], axis=2)
    above = jnp.concatenate([center[:, :, 1:], high.astype(jnp.float32)], axis=2)
    total = total + above + below
    z_padded = jnp.pad(center, ((0, 0), (0, 0), (0, 0), (1, 1)))
    total = total + z_padded[..., 2:] + z_padded[..., :-2]
    keep = live.astype(jnp.float32)[:, :, None, None]
    applied = ((-0.5 * total + grid_potential[None] * center) * keep).astype(jnp.bfloat16)
    applied_data = lax.all_to_all(applied, "region", split_axis=1, concat_axis=0, tiled=True)

    flat = (func_count * region_count, -1)
    blocks = pair_blocks(pair_list, data.reshape(flat), applied_data.reshape(flat))
    listed = pair_list.shape[0] // pair_axis
    width = W // region_count
    parts = blocks.reshape(pair_axis, listed, 2, W, W)
    parts = lax.all_to_all(parts, "pair", split_axis=0, concat_axis=0, tiled=True)
    sums = jnp.sum(parts, axis=0)
    sums = sums.reshape(listed, 2, region_count, width, W).transpose(2, 1, 0, 3, 4)
    sums = lax.all_to_all(sums, "region", split_axis=0, concat_axis=0, tiled=True)
    result = jnp.sum(sums, axis=0).reshape(2, listed, width * W)
    return result[0], result[1], applied


def solution(mesh):
    in_specs = (P("region", None, "pair", None), P("region", "pair", None), P(), P())
    out_specs = (P("pair", "region"), P("pair", "region"), P("region", None, "pair", None))
    return jax.shard_map(local, mesh=mesh, in_specs=in_specs, out_specs=out_specs, check_vma=False)
```

```python
import jax
import jax.numpy as jnp
from jax import lax
from jax.experimental import pallas as pl
from jax.experimental.pallas import tpu as pltpu
from jax.sharding import PartitionSpec as P

W = 128


def pair_kernel(pairs_ref, data_ref, right_ref, out_ref):
    contract = (((1,), (1,)), ((), ()))

    def step(k, carry):
        left = data_ref[pl.ds(pl.multiple_of(pairs_ref[k, 0] * W, W), W), :]
        rows = pl.ds(pl.multiple_of(pairs_ref[k, 1] * W, W), W)
        right = right_ref[rows, :]
        out_ref[k] = lax.dot_general(left, right, contract, preferred_element_type=jnp.float32)
        return carry

    lax.fori_loop(0, pairs_ref.shape[0], step, 0)


def pair_blocks(pair_list, data, right):
    count = pair_list.shape[0]
    return pl.pallas_call(
        pair_kernel,
        out_shape=jax.ShapeDtypeStruct((count, W, W), jnp.float32),
        in_specs=[
            pl.BlockSpec(memory_space=pltpu.SMEM),
            pl.BlockSpec(memory_space=pltpu.VMEM),
            pl.BlockSpec(memory_space=pltpu.VMEM),
        ],
        out_specs=pl.BlockSpec(memory_space=pltpu.VMEM),
        compiler_params=pltpu.CompilerParams(vmem_limit_bytes=32 * 2**20),
        cost_estimate=pl.CostEstimate(
            flops=count * 2 * W * W * data.shape[1],
            bytes_accessed=data.size * 4 + count * 4 * W * W,
            transcendentals=0,
        ),
    )(pair_list, data, right)


def halved(parts, bit):
    count = lax.axis_size("pair")
    mine = (lax.axis_index("pair") // bit) % 2
    kept = lax.dynamic_index_in_dim(parts, mine, 0, keepdims=False)
    given = lax.dynamic_index_in_dim(parts, 1 - mine, 0, keepdims=False)
    return kept + lax.ppermute(given, "pair", [(i, i ^ bit) for i in range(count)])


def reduced(blocks):
    count = lax.axis_size("pair")
    region_count = lax.axis_size("region")
    listed = blocks.shape[0] // count
    parts = blocks.reshape(count, listed, W, W)
    bit = 1
    while bit < count:
        rest = parts.shape[0] // 2
        parts = parts.reshape(rest, 2, listed, W, W).swapaxes(0, 1)
        parts = halved(parts, bit)
        bit *= 2
    width = W // region_count
    sums = parts.reshape(listed, region_count, width, W).swapaxes(0, 1)
    sums = lax.all_to_all(sums, "region", split_axis=0, concat_axis=0, tiled=True)
    return jnp.sum(sums, axis=0).reshape(listed, width * W)


def local(phi, potential, pair_list, support):
    region_id = lax.axis_index("region")
    region_count = lax.axis_size("region")
    pair_axis = lax.axis_size("pair")
    func_count, _, row_count, depth = phi.shape
    owners = (region_id * func_count + jnp.arange(func_count)) // W
    live = support[owners]
    confined = jnp.where((live > 0)[:, :, None, None], phi, jnp.zeros_like(phi))
    forward = [(i, (i + 1) % pair_axis) for i in range(pair_axis)]
    backward = [(target, source) for source, target in forward]
    low = lax.ppermute(confined[:, :, -1:], "pair", forward)
    high = lax.ppermute(confined[:, :, :1], "pair", backward)
    grid_potential = lax.all_gather(potential, "region", axis=0, tiled=True)
    low, high, grid_potential, sent = lax.optimization_barrier(
        (low, high, grid_potential, confined)
    )
    data = lax.all_to_all(sent, "region", split_axis=1, concat_axis=0, tiled=True)

    center = confined.astype(jnp.float32)
    total = jnp.roll(center, -1, axis=1) + jnp.roll(center, 1, axis=1) - 6.0 * center
    below = jnp.concatenate([low.astype(jnp.float32), center[:, :, :-1]], axis=2)
    above = jnp.concatenate([center[:, :, 1:], high.astype(jnp.float32)], axis=2)
    total = total + above + below
    z_padded = jnp.pad(center, ((0, 0), (0, 0), (0, 0), (1, 1)))
    total = total + z_padded[..., 2:] + z_padded[..., :-2]
    keep = live.astype(jnp.float32)[:, :, None, None]
    applied = ((-0.5 * total + grid_potential[None] * center) * keep).astype(jnp.bfloat16)
    applied_data = lax.all_to_all(applied, "region", split_axis=1, concat_axis=0, tiled=True)

    flat = (func_count * region_count, -1)
    data = data.reshape(flat)
    applied_data = applied_data.reshape(flat)
    intersection = reduced(pair_blocks(pair_list, data, data))
    hamiltonian = reduced(pair_blocks(pair_list, data, applied_data))
    return intersection, hamiltonian, applied


def solution(mesh):
    in_specs = (P("region", None, "pair", None), P("region", "pair", None), P(), P())
    out_specs = (P("pair", "region"), P("pair", "region"), P("region", None, "pair", None))
    return jax.shard_map(local, mesh=mesh, in_specs=in_specs, out_specs=out_specs, check_vma=False)
```

```python
import jax
import jax.numpy as jnp
from jax import lax
from jax.experimental import pallas as pl
from jax.experimental.pallas import tpu as pltpu
from jax.sharding import PartitionSpec as P

W = 128


def pair_kernel(pairs_ref, data_ref, right_ref, out_ref):
    contract = (((1,), (1,)), ((), ()))

    def step(k, carry):
        left = data_ref[pl.ds(pl.multiple_of(pairs_ref[k, 0] * W, W), W), :]
        rows = pl.ds(pl.multiple_of(pairs_ref[k, 1] * W, W), W)
        right = right_ref[rows, :]
        out_ref[k] = lax.dot_general(left, right, contract, preferred_element_type=jnp.float32)
        return carry

    lax.fori_loop(0, pairs_ref.shape[0], step, 0)


def pair_blocks(pair_list, data, right):
    count = pair_list.shape[0]
    return pl.pallas_call(
        pair_kernel,
        out_shape=jax.ShapeDtypeStruct((count, W, W), jnp.float32),
        in_specs=[
            pl.BlockSpec(memory_space=pltpu.SMEM),
            pl.BlockSpec(memory_space=pltpu.VMEM),
            pl.BlockSpec(memory_space=pltpu.VMEM),
        ],
        out_specs=pl.BlockSpec(memory_space=pltpu.VMEM),
        compiler_params=pltpu.CompilerParams(vmem_limit_bytes=32 * 2**20),
        cost_estimate=pl.CostEstimate(
            flops=count * 2 * W * W * data.shape[1],
            bytes_accessed=data.size * 4 + count * 4 * W * W,
            transcendentals=0,
        ),
    )(pair_list, data, right)


def gathered(block):
    count = lax.axis_size("region")
    index = lax.axis_index("region")
    bit = 1
    while bit < count:
        other = lax.ppermute(block, "region", [(i, i ^ bit) for i in range(count)])
        upper = (index // bit) % 2 == 1
        block = jnp.concatenate(
            [jnp.where(upper, other, block), jnp.where(upper, block, other)], axis=0
        )
        bit *= 2
    return block


def halved(parts, bit):
    count = lax.axis_size("pair")
    mine = (lax.axis_index("pair") // bit) % 2
    kept = lax.dynamic_index_in_dim(parts, mine, 0, keepdims=False)
    given = lax.dynamic_index_in_dim(parts, 1 - mine, 0, keepdims=False)
    return kept + lax.ppermute(given, "pair", [(i, i ^ bit) for i in range(count)])


def reduced(blocks):
    count = lax.axis_size("pair")
    region_count = lax.axis_size("region")
    listed = blocks.shape[0] // count
    parts = blocks.reshape(count, listed, W, W)
    bit = 1
    while bit < count:
        rest = parts.shape[0] // 2
        parts = parts.reshape(rest, 2, listed, W, W).swapaxes(0, 1)
        parts = halved(parts, bit)
        bit *= 2
    width = W // region_count
    sums = parts.reshape(listed, region_count, width, W).swapaxes(0, 1)
    sums = lax.all_to_all(sums, "region", split_axis=0, concat_axis=0, tiled=True)
    return jnp.sum(sums, axis=0).reshape(listed, width * W)


def local(phi, potential, pair_list, support):
    region_id = lax.axis_index("region")
    region_count = lax.axis_size("region")
    pair_axis = lax.axis_size("pair")
    func_count, _, row_count, depth = phi.shape
    owners = (region_id * func_count + jnp.arange(func_count)) // W
    live = support[owners]
    confined = jnp.where((live > 0)[:, :, None, None], phi, jnp.zeros_like(phi))
    forward = [(i, (i + 1) % pair_axis) for i in range(pair_axis)]
    backward = [(target, source) for source, target in forward]
    low = lax.ppermute(confined[:, :, -1:], "pair", forward)
    high = lax.ppermute(confined[:, :, :1], "pair", backward)
    grid_potential = gathered(potential)
    low, high, grid_potential, sent = lax.optimization_barrier(
        (low, high, grid_potential, confined)
    )
    data = lax.all_to_all(sent, "region", split_axis=1, concat_axis=0, tiled=True)

    center = confined.astype(jnp.float32)
    total = jnp.roll(center, -1, axis=1) + jnp.roll(center, 1, axis=1) - 6.0 * center
    below = jnp.concatenate([low.astype(jnp.float32), center[:, :, :-1]], axis=2)
    above = jnp.concatenate([center[:, :, 1:], high.astype(jnp.float32)], axis=2)
    total = total + above + below
    z_padded = jnp.pad(center, ((0, 0), (0, 0), (0, 0), (1, 1)))
    total = total + z_padded[..., 2:] + z_padded[..., :-2]
    keep = live.astype(jnp.float32)[:, :, None, None]
    applied = ((-0.5 * total + grid_potential[None] * center) * keep).astype(jnp.bfloat16)
    data, applied_sent = lax.optimization_barrier((data, applied))
    applied_data = lax.all_to_all(applied_sent, "region", split_axis=1, concat_axis=0, tiled=True)

    flat = (func_count * region_count, -1)
    data = data.reshape(flat)
    applied_data = applied_data.reshape(flat)
    intersection = reduced(pair_blocks(pair_list, data, data))
    hamiltonian = reduced(pair_blocks(pair_list, data, applied_data))
    return intersection, hamiltonian, applied


def solution(mesh):
    in_specs = (P("region", None, "pair", None), P("region", "pair", None), P(), P())
    out_specs = (P("pair", "region"), P("pair", "region"), P("region", None, "pair", None))
    return jax.shard_map(local, mesh=mesh, in_specs=in_specs, out_specs=out_specs, check_vma=False)
```

```python
import jax
import jax.numpy as jnp
from jax import lax
from jax.experimental import pallas as pl
from jax.experimental.pallas import tpu as pltpu
from jax.sharding import PartitionSpec as P

W = 128


def pair_kernel(pairs_ref, data_ref, right_ref, out_ref):
    contract = (((1,), (1,)), ((), ()))

    def step(k, carry):
        left = data_ref[pl.ds(pl.multiple_of(pairs_ref[k, 0] * W, W), W), :]
        rows = pl.ds(pl.multiple_of(pairs_ref[k, 1] * W, W), W)
        right = right_ref[rows, :]
        out_ref[k] = lax.dot_general(left, right, contract, preferred_element_type=jnp.float32)
        return carry

    lax.fori_loop(0, pairs_ref.shape[0], step, 0)


def pair_blocks(pair_list, data, right):
    count = pair_list.shape[0]
    return pl.pallas_call(
        pair_kernel,
        out_shape=jax.ShapeDtypeStruct((count, W, W), jnp.float32),
        in_specs=[
            pl.BlockSpec(memory_space=pltpu.SMEM),
            pl.BlockSpec(memory_space=pltpu.VMEM),
            pl.BlockSpec(memory_space=pltpu.VMEM),
        ],
        out_specs=pl.BlockSpec(memory_space=pltpu.VMEM),
        compiler_params=pltpu.CompilerParams(vmem_limit_bytes=32 * 2**20),
        cost_estimate=pl.CostEstimate(
            flops=count * 2 * W * W * data.shape[1],
            bytes_accessed=data.size * 4 + count * 4 * W * W,
            transcendentals=0,
        ),
    )(pair_list, data, right)


def gathered(block):
    count = lax.axis_size("region")
    index = lax.axis_index("region")
    bit = 1
    while bit < count:
        other = lax.ppermute(block, "region", [(i, i ^ bit) for i in range(count)])
        upper = (index // bit) % 2 == 1
        block = jnp.concatenate(
            [jnp.where(upper, other, block), jnp.where(upper, block, other)], axis=0
        )
        bit *= 2
    return block


def halved(parts, bit):
    count = lax.axis_size("pair")
    mine = (lax.axis_index("pair") // bit) % 2
    kept = lax.dynamic_index_in_dim(parts, mine, 0, keepdims=False)
    given = lax.dynamic_index_in_dim(parts, 1 - mine, 0, keepdims=False)
    return kept + lax.ppermute(given, "pair", [(i, i ^ bit) for i in range(count)])


def pair_reduced(blocks):
    count = lax.axis_size("pair")
    listed = blocks.shape[0] // count
    parts = blocks.reshape(count, listed, W, W)
    bit = 1
    while bit < count:
        rest = parts.shape[0] // 2
        parts = parts.reshape(rest, 2, listed, W, W).swapaxes(0, 1)
        parts = halved(parts, bit)
        bit *= 2
    return parts


def region_reduced(parts):
    region_count = lax.axis_size("region")
    listed = parts.size // (W * W)
    width = W // region_count
    sums = parts.reshape(listed, region_count, width, W).swapaxes(0, 1)
    sums = lax.all_to_all(sums, "region", split_axis=0, concat_axis=0, tiled=True)
    return jnp.sum(sums, axis=0).reshape(listed, width * W)


def local(phi, potential, pair_list, support):
    region_id = lax.axis_index("region")
    region_count = lax.axis_size("region")
    pair_axis = lax.axis_size("pair")
    func_count, _, row_count, depth = phi.shape
    owners = (region_id * func_count + jnp.arange(func_count)) // W
    live = support[owners]
    confined = jnp.where((live > 0)[:, :, None, None], phi, jnp.zeros_like(phi))
    forward = [(i, (i + 1) % pair_axis) for i in range(pair_axis)]
    backward = [(target, source) for source, target in forward]
    low = lax.ppermute(confined[:, :, -1:], "pair", forward)
    high = lax.ppermute(confined[:, :, :1], "pair", backward)
    grid_potential = gathered(potential)
    low, high, grid_potential, sent = lax.optimization_barrier(
        (low, high, grid_potential, confined)
    )
    data = lax.all_to_all(sent, "region", split_axis=1, concat_axis=0, tiled=True)

    center = confined.astype(jnp.float32)
    total = jnp.roll(center, -1, axis=1) + jnp.roll(center, 1, axis=1) - 6.0 * center
    below = jnp.concatenate([low.astype(jnp.float32), center[:, :, :-1]], axis=2)
    above = jnp.concatenate([center[:, :, 1:], high.astype(jnp.float32)], axis=2)
    total = total + above + below
    z_padded = jnp.pad(center, ((0, 0), (0, 0), (0, 0), (1, 1)))
    total = total + z_padded[..., 2:] + z_padded[..., :-2]
    keep = live.astype(jnp.float32)[:, :, None, None]
    applied = ((-0.5 * total + grid_potential[None] * center) * keep).astype(jnp.bfloat16)
    data, applied_sent = lax.optimization_barrier((data, applied))
    applied_data = lax.all_to_all(applied_sent, "region", split_axis=1, concat_axis=0, tiled=True)

    flat = (func_count * region_count, -1)
    data = data.reshape(flat)
    applied_data = applied_data.reshape(flat)
    shares = pair_reduced(pair_blocks(pair_list, data, data))
    shares, applied_data = lax.optimization_barrier((shares, applied_data))
    intersection = region_reduced(shares)
    hamiltonian = region_reduced(pair_reduced(pair_blocks(pair_list, data, applied_data)))
    return intersection, hamiltonian, applied


def solution(mesh):
    in_specs = (P("region", None, "pair", None), P("region", "pair", None), P(), P())
    out_specs = (P("pair", "region"), P("pair", "region"), P("region", None, "pair", None))
    return jax.shard_map(local, mesh=mesh, in_specs=in_specs, out_specs=out_specs, check_vma=False)
```
